32 devices in a mesh: expert: 16 (over z, y, x), wshard: 2 (over core).
Axes of the slice: x: 2, y: 2, z: 4, core: 2. Of those that a mesh axis runs over, the one named last changes fastest.
Arguments:
- tokens: bfloat16 [12288, 768], P(('expert', 'wshard')), may hold values from -6 to 6
- norm1_gain: bfloat16 [768], P('wshard'), may hold values from 0.5 to 1.5
- w_query: bfloat16 [768, 768], P('wshard'), may hold values from -0.21875 to 0.21875
- w_key: bfloat16 [768, 768], P('wshard'), may hold values from -0.21875 to 0.21875
- w_value: bfloat16 [768, 768], P('wshard'), may hold values from -0.21875 to 0.21875
- w_output: bfloat16 [768, 768], P('wshard'), may hold values from -1.25 to 1.25
- rel_bias: bfloat16 [32, 12], P('wshard'), may hold values from -4 to 4
- norm2_gain: bfloat16 [768], P('wshard'), may hold values from 0.5 to 1.5
- w_router: bfloat16 [768, 16], P('wshard'), may hold values from -0.15625 to 0.15625
- w_in: bfloat16 [16, 768, 3072], P('expert', None, 'wshard'), may hold values from -0.21875 to 0.21875
- w_out: bfloat16 [16, 3072, 768], P('expert', 'wshard'), may hold values from -2.5 to 2.5
- seq_lens: int32 [32, 3], P(('expert', 'wshard')), may hold values from 1 to 256, 384 in all within a row
- routes: int32 [12288, 1], P(('expert', 'wshard')), may hold values from 0 to 15; in each aligned block of 384 rows (0 to 383, 384 to 767, ...) at most 36 rows name the same one
- cotangent: bfloat16 [12288, 768], P(('expert', 'wshard')), may hold values from -6 to 6
Outputs:
- block_out: bfloat16 [12288, 768], P(('expert', 'wshard'))
- grad_tokens: float32 [12288, 768], P(('expert', 'wshard'))
- grad_norm1: float32 [768], P('wshard')
- grad_query: float32 [768, 768], P('wshard')
- grad_key: float32 [768, 768], P('wshard')
- grad_value: float32 [768, 768], P('wshard')
- grad_output: float32 [768, 768], P('wshard')
- grad_bias: float32 [32, 12], P('wshard')
- grad_norm2: float32 [768], P('wshard')
- grad_router: float32 [768, 16], P('wshard')
- grad_w_in: float32 [16, 768, 3072], P('expert', None, 'wshard')
- grad_w_out: float32 [16, 3072, 768], P('expert', 'wshard')
The draws below stay inside these ranges and needn't reach their ends.
Inputs may be any that keep to these rules, and one draw needn't show every extreme that they name: `routes`: on the rows of one device no expert is named by more than 36 rows. `seq_lens`: the 3 lengths of a device add up to 384.
All inputs are finite; a program needn't handle non-finite values.
Results may differ from the reference program's by a relative error of at most 0.015.
Values may be sent and summed in bfloat16 or wider, within the bound.
A program may use at most 192 MiB of HBM per device.

```python
import math
import jax
import jax.numpy as jnp
import numpy as np
from jax import lax

D = 768
HEADS = 12
HEAD_DIM = 64
FF = 3072
NUM_BUCKETS = 32
SEQS_DEV = 3
ROWS = 384
MAXLEN = 256
EXPERTS = 16
CAP = 36
TOKENS = 12288
DEVICES = 32


def block_scale(own_key, extent, pieces, least, top_value):
    level = 1.0
    for position, parts in pieces:
        steps = jax.random.uniform(jax.random.fold_in(jax.random.fold_in(own_key, 6), position), (parts,), jnp.float32, least / len(pieces), top_value / len(pieces))
        level = level * jnp.repeat(jnp.exp(steps), extent[position] // parts).reshape((-1,) + (1,) * (len(extent) - 1 - position))
    return level


def profile(number_of, total, reach, lean):
    weights = [(1 << 20) // math.isqrt(rank ** lean) + 1 for rank in range(2, number_of + 1)]
    spare, given = total - reach - (number_of - 1), [1] * (number_of - 1)
    while spare > 0:
        movable = [i for i in range(number_of - 1) if given[i] < reach]
        whole, left = sum([weights[i] for i in movable]), spare
        for i in movable:
            addition = min(reach - given[i], max(1, left * weights[i] // whole), spare)
            given[i] = given[i] + addition
            spare = spare - addition
    return np.array([reach] + given)


def uneven_parts(own_key, number_of, total, most, slope):
    if number_of == 2:
        one = jax.random.randint(own_key, (), max(1, total - most), min(most, total - 1) + 1)
        return jnp.stack([one, total - one])
    sizes = jnp.asarray(profile(number_of, total, most, slope), jnp.int32)
    twos = (number_of - 1) // 2
    donor, taker = sizes[1:1 + 2 * twos:2], sizes[2:2 + 2 * twos:2]
    slack = jnp.minimum(donor - 1, most - taker)
    shifted = jax.random.randint(jax.random.fold_in(own_key, 1), (twos,), 0, 1 << 20) % (slack + 1)
    sizes = sizes.at[1:1 + 2 * twos:2].set(donor - shifted).at[2:2 + 2 * twos:2].set(taker + shifted)
    return sizes[jax.random.permutation(jax.random.fold_in(own_key, 2), number_of)]


def deal_out(own_key, own, number, rows, number_of, top, bound, skew):
    order = jax.random.permutation(own_key, number_of)
    heavy_load, ordinary = shares(number_of, rows * top, bound, skew, True), shares(number_of, rows * top, bound, skew, False)
    places = jnp.arange(number_of)

    def named(sizes, offset_by):
        used = int((sizes > 0).sum())
        fixed = max(1, used // 4)
        shifted = fixed + (places - fixed + offset_by * (used - fixed)) % max(1, number_of - fixed)
        return jnp.zeros((number_of,), jnp.int32).at[order[jnp.where(places < fixed, places, shifted)]].set(jnp.asarray(sizes, jnp.int32))

    sizes = jnp.where(number % 4 == 0, named(heavy_load, number // 4), named(ordinary, number - number // 4 - 1))
    mixed = jax.random.permutation(jax.random.fold_in(own, 3), number_of)
    donor, sink = mixed[0:number_of // 2 * 2:2], mixed[1:number_of // 2 * 2:2]
    margin = jnp.minimum(sizes[donor] - 1, bound - sizes[sink]) // 2
    margin = jnp.where((donor == order[0]) | (sink == order[0]) | (sizes[sink] == 0), 0, jnp.maximum(margin, 0))
    shifted = jax.random.randint(jax.random.fold_in(own, 4), (number_of // 2,), 0, 1 << 20) % (margin + 1)
    sizes = sizes.at[donor].add(-shifted).at[sink].add(shifted)
    items = jnp.searchsorted(jnp.cumsum(sizes), jnp.arange(rows * top), side="right").astype(jnp.int32)
    listing = items.reshape(top, rows).T
    listing = listing[jax.random.permutation(jax.random.fold_in(own, 1), rows)]
    offset_by = jax.random.randint(jax.random.fold_in(own, 2), (rows, 1), 0, top)
    return jnp.take_along_axis(listing, (jnp.arange(top)[None, :] + offset_by) % top, axis=1)


def shares(count, total, most, slope, full):
    loads = [(1 << 20) // math.isqrt(rank ** slope) + 1 for rank in range(1, count + 1)]
    largest = most if full else min(most, max(-(-total // count), total * loads[0] // sum(loads)))
    least = 1 if total - largest >= count - 1 else 0
    given, rest = [largest] + [least] * (count - 1), total - largest - least * (count - 1)
    while rest > 0:
        free = [i for i in range(1, count) if given[i] < largest] or [i for i in range(1, count) if given[i] < most]
        pool, left = sum([loads[i] for i in free]), rest
        for i in free:
            more = min(most - given[i], max(1, left * loads[i] // pool), rest)
            given[i] = given[i] + more
            rest = rest - more
    return np.array(given)


def noise(own_key, shape, spread, most, split=(), kind=jnp.bfloat16):
    array = jax.random.normal(own_key, shape, jnp.float32) * spread
    if len(split) > 0:
        array = block_scale(own_key, shape, split, -0.22, 0.18) * array
    return jnp.clip(array, min=-most, max=most).astype(kind)


def setup_inputs(seed: int = 0) -> dict:
    arg_keys = jax.random.split(jax.random.key(seed), 15)
    tokens = noise(arg_keys[0], (TOKENS, D), 1.0, 6.0, ((0, 32),))
    norm1_gain = jnp.clip(1.0 + 0.1 * jax.random.normal(arg_keys[1], (D,), jnp.float32), 0.5, 1.5).astype(jnp.bfloat16)
    w_query = noise(arg_keys[2], (D, D), D ** -0.5, 0.21875, ((0, 2),))
    w_key = noise(arg_keys[3], (D, D), D ** -0.5, 0.21875, ((0, 2),))
    w_value = noise(arg_keys[4], (D, D), D ** -0.5, 0.21875, ((0, 2),))
    w_output = noise(arg_keys[5], (D, D), (max(1, D // 32)) ** -0.5, 1.25, ((0, 2),))
    rel_bias = noise(arg_keys[6], (NUM_BUCKETS, HEADS), 1.0, 4.0, ((0, 2),))
    norm2_gain = jnp.clip(1.0 + 0.1 * jax.random.normal(arg_keys[7], (D,), jnp.float32), 0.5, 1.5).astype(jnp.bfloat16)
    w_router = noise(arg_keys[8], (D, EXPERTS), (2 * D) ** -0.5, 0.15625, ((0, 2),))
    w_in = noise(arg_keys[9], (EXPERTS, D, FF), D ** -0.5, 0.21875, ((0, 16), (2, 2)))
    w_out = noise(arg_keys[10], (EXPERTS, FF, D), (1.5 * EXPERTS * FF ** -0.5), 2.5, ((0, 16), (1, 2)))
    seq_lens = jax.vmap(lambda own: uneven_parts(own, SEQS_DEV, ROWS, MAXLEN, 2))(jax.random.split(arg_keys[11], DEVICES)).reshape((DEVICES, SEQS_DEV)).astype(jnp.int32)
    routes_keys = jax.random.split(jax.random.fold_in(arg_keys[12], 1), TOKENS // ROWS)
    routes_turns = jax.random.permutation(jax.random.fold_in(arg_keys[12], 3), TOKENS // ROWS)
    routes = jax.vmap(lambda own, number: deal_out(jax.random.fold_in(arg_keys[12], 2), own, number, ROWS, EXPERTS, 1, CAP, 2))(routes_keys, routes_turns).reshape((TOKENS, 1))
    cotangent = noise(arg_keys[13], (TOKENS, D), 1.0, 6.0, ((0, 32),))
    return dict(tokens=tokens, norm1_gain=norm1_gain, w_query=w_query, w_key=w_key, w_value=w_value, w_output=w_output, rel_bias=rel_bias, norm2_gain=norm2_gain, w_router=w_router, w_in=w_in, w_out=w_out, seq_lens=seq_lens, routes=routes, cotangent=cotangent)


@jax.custom_vjp
def low(v):
    return lax.optimization_barrier(v.astype(jnp.bfloat16)).astype(jnp.float32)

@jax.custom_vjp
def low_back(v):
    return v

def low_keep(v):
    return (low(v), None)

def low_pass(kept, grad):
    return (grad,)

def back_keep(v):
    return (v, None)

def back_low(kept, grad):
    return (low(grad),)
low.defvjp(low_keep, low_pass)
low_back.defvjp(back_keep, back_low)
bucket_edges = (12, 16, 23, 32, 46, 64, 91)
mask_fill = -1e+30
norm_eps = 1e-06
highest = lax.Precision.HIGHEST

def both_ways(value):
    return low(low_back(value))

def rms_scale(value, gain):
    return value * lax.rsqrt(lax.optimization_barrier(jnp.mean(value * value, axis=-1, keepdims=True)) + norm_eps) * gain

def smooth(value):
    return jax.nn.gelu(value, approximate=True)

def bucket_grid(length):
    query_pos = lax.broadcasted_iota(jnp.int32, (length, length), 0)
    memory_pos = lax.broadcasted_iota(jnp.int32, (length, length), 1)
    offset = memory_pos - query_pos
    distance = jnp.abs(offset)
    beyond = 8 + sum(((distance >= edge).astype(jnp.int32) for edge in bucket_edges))
    upper = jnp.where(offset > 0, 16, 0).astype(jnp.int32)
    return (upper + jnp.where(distance < 8, distance, beyond)).astype(jnp.int32)

def segment_of(lengths, length):
    ends = jnp.cumsum(lengths).astype(jnp.int32)
    places = lax.broadcasted_iota(jnp.int32, (length, 1), 0)
    return lax.optimization_barrier(jnp.sum((places >= ends[None, :]).astype(jnp.int32), axis=1)).astype(jnp.int32)

def forward(tokens, norm1_gain, w_query, w_key, w_value, w_output, rel_bias, norm2_gain, w_router, w_in, w_out, seq_lens, routes):
    grid = bucket_grid(ROWS)
    factor = HEAD_DIM ** (-0.5)

    def mixer(block):
        inputs, lengths = block
        normed = low(rms_scale(inputs, norm1_gain))
        query = both_ways(jnp.dot(normed, w_query, precision=highest)).reshape(ROWS, HEADS, HEAD_DIM)
        key = both_ways(jnp.dot(normed, w_key, precision=highest)).reshape(ROWS, HEADS, HEAD_DIM)
        value = both_ways(jnp.dot(normed, w_value, precision=highest)).reshape(ROWS, HEADS, HEAD_DIM)
        segment = segment_of(lengths, ROWS)
        same = segment[:, None] == segment[None, :]
        position_bias = jnp.transpose(rel_bias[grid], (2, 0, 1))
        scores = jnp.einsum('ihd,jhd->hij', query, key, precision=highest) * factor + position_bias
        scores = low_back(jnp.where(same[None], scores, mask_fill))
        weights = low(jax.nn.softmax(scores, axis=-1))
        attended = jnp.einsum('hij,jhd->ihd', weights, value, precision=highest).reshape(ROWS, D)
        attended = both_ways(attended)
        return inputs + low_back(jnp.dot(attended, w_output, precision=highest))
    hidden = lax.map(jax.checkpoint(mixer), (tokens.reshape(DEVICES, ROWS, D), seq_lens)).reshape(TOKENS, D)
    normed = low(rms_scale(hidden, norm2_gain))
    logits = low_back(jnp.dot(normed, w_router, precision=highest))
    chances = jax.nn.softmax(logits, axis=-1)
    chosen = routes[:, 0].astype(jnp.int32)
    picks = chosen[:, None] == lax.broadcasted_iota(jnp.int32, (1, EXPERTS), 1)
    gate = lax.optimization_barrier(jnp.sum(jnp.where(picks, chances, 0.0), axis=1, keepdims=True))
    counted = picks.astype(jnp.int32).reshape(DEVICES, ROWS, EXPERTS)
    earlier = jnp.cumsum(counted, axis=1).astype(jnp.int32) - counted
    slots = lax.optimization_barrier(jnp.sum(earlier * counted, axis=2)).astype(jnp.int32).reshape(TOKENS)
    device = lax.broadcasted_iota(jnp.int32, (TOKENS,), 0) // ROWS
    place = ((chosen * DEVICES + device) * CAP + slots).astype(jnp.int32)
    sent = low_back(normed)
    buffer = jnp.zeros((EXPERTS * DEVICES * CAP, D), jnp.float32).at[place].set(sent)
    buffer = buffer.reshape(EXPERTS, DEVICES * CAP, D)

    def expert(block):
        arrived, inner, outer = block
        before = low_back(jnp.dot(arrived, inner, precision=highest))
        return jnp.dot(low(smooth(before)), outer, precision=highest)
    results = lax.map(jax.checkpoint(expert), (buffer, w_in, w_out)).reshape(EXPERTS * DEVICES * CAP, D)
    returned = both_ways(results[place])
    return hidden + gate * returned

def reference(tokens, norm1_gain, w_query, w_key, w_value, w_output, rel_bias, norm2_gain, w_router, w_in, w_out, seq_lens, routes, cotangent):
    floats = (tokens.astype(jnp.float32), norm1_gain.astype(jnp.float32), w_query.astype(jnp.float32), w_key.astype(jnp.float32), w_value.astype(jnp.float32), w_output.astype(jnp.float32), rel_bias.astype(jnp.float32), norm2_gain.astype(jnp.float32), w_router.astype(jnp.float32), w_in.astype(jnp.float32), w_out.astype(jnp.float32))

    def wrapped(*values):
        return forward(*values, seq_lens, routes)
    output, pullback = jax.vjp(wrapped, *floats)
    grads = pullback(cotangent.astype(jnp.float32))
    return (output.astype(jnp.bfloat16), grads[0], grads[1], grads[2], grads[3], grads[4], grads[5], grads[6], grads[7], grads[8], grads[9], grads[10])
```

```python
import jax
import jax.numpy as jnp
from jax import lax
from jax.sharding import PartitionSpec as P

bucket_edges = (12, 16, 23, 32, 46, 64, 91)
mask_fill = -1e30
norm_eps = 1e-06


def rms_scale(value, gain):
    return value * lax.rsqrt(jnp.mean(value * value, axis=-1, keepdims=True) + norm_eps) * gain


def smooth(value):
    return jax.nn.gelu(value, approximate=True)


def matmul(left, right):
    return jnp.dot(left, right, preferred_element_type=jnp.float32)


def times_transposed(left, right):
    return lax.dot_general(
        left, right, (((1,), (1,)), ((), ())), preferred_element_type=jnp.float32
    )


def transposed_times(left, right):
    return lax.dot_general(
        left, right, (((0,), (0,)), ((), ())), preferred_element_type=jnp.float32
    )


def bucket_grid(length):
    query_pos = lax.broadcasted_iota(jnp.int32, (length, length), 0)
    memory_pos = lax.broadcasted_iota(jnp.int32, (length, length), 1)
    offset = memory_pos - query_pos
    distance = jnp.abs(offset)
    beyond = 8 + sum(((distance >= edge).astype(jnp.int32) for edge in bucket_edges))
    upper = jnp.where(offset > 0, 16, 0).astype(jnp.int32)
    return upper + jnp.where(distance < 8, distance, beyond)


def segment_of(lengths, length):
    count = lengths.shape[0]
    upto = lax.broadcasted_iota(jnp.int32, (count, count), 0) <= lax.broadcasted_iota(
        jnp.int32, (count, count), 1
    )
    ends = jnp.sum(jnp.where(upto, lengths[:, None], 0), axis=0)
    places = lax.broadcasted_iota(jnp.int32, (length, 1), 0)
    return jnp.sum((places >= ends[None, :]).astype(jnp.int32), axis=1)


def per_device(
    tokens,
    norm1_gain,
    w_query,
    w_key,
    w_value,
    w_output,
    rel_bias,
    norm2_gain,
    w_router,
    w_in,
    w_out,
    seq_lens,
    routes,
    cotangent,
):
    gathered = (
        lax.all_gather(norm1_gain, "wshard", axis=0, tiled=True),
        lax.all_gather(w_query, "wshard", axis=0, tiled=True),
        lax.all_gather(w_key, "wshard", axis=0, tiled=True),
        lax.all_gather(w_value, "wshard", axis=0, tiled=True),
        lax.all_gather(w_output, "wshard", axis=0, tiled=True),
        lax.all_gather(rel_bias, "wshard", axis=0, tiled=True),
        lax.all_gather(norm2_gain, "wshard", axis=0, tiled=True),
        lax.all_gather(w_router, "wshard", axis=0, tiled=True),
    )
    (
        gain_first,
        query_weight,
        key_weight,
        value_weight,
        output_weight,
        bias_table,
        gain_second,
        router_weight,
    ) = gathered
    gain_first = gain_first.astype(jnp.float32)
    gain_second = gain_second.astype(jnp.float32)
    length, width = tokens.shape
    buckets, heads = bias_table.shape
    head_size = width // heads
    factor = head_size ** (-0.5)
    experts = router_weight.shape[1]
    capacity = max(2, 3 * length // (2 * experts))
    inputs = tokens.astype(jnp.float32)
    grid = bucket_grid(length)
    bucket_hits = (grid[None] == lax.broadcasted_iota(jnp.int32, (buckets, 1, 1), 0)).astype(
        jnp.bfloat16
    )
    segment = segment_of(seq_lens[0], length)
    same = (segment[:, None] == segment[None, :])[None]
    position_bias = jnp.einsum(
        "bij,bh->hij", bucket_hits, bias_table, preferred_element_type=jnp.float32
    )
    normed_first = rms_scale(inputs, gain_first).astype(jnp.bfloat16)
    query_low = (
        matmul(normed_first, query_weight).astype(jnp.bfloat16).reshape(length, heads, head_size)
    )
    key_low = (
        matmul(normed_first, key_weight).astype(jnp.bfloat16).reshape(length, heads, head_size)
    )
    value_low = (
        matmul(normed_first, value_weight).astype(jnp.bfloat16).reshape(length, heads, head_size)
    )

    def score_of():
        raw = (
            jnp.einsum("ihd,jhd->hij", query_low, key_low, preferred_element_type=jnp.float32)
            * factor
            + position_bias
        )
        return jnp.where(same, raw, mask_fill)

    scores = score_of()
    peak = jnp.max(scores, axis=-1, keepdims=True)
    lifted = jnp.exp(scores - peak)
    totals_row = jnp.sum(lifted, axis=-1, keepdims=True)
    probs = lifted / totals_row
    log_total = peak + jnp.log(totals_row)
    probs_low = probs.astype(jnp.bfloat16)
    attended = jnp.einsum("hij,jhd->ihd", probs_low, value_low, preferred_element_type=jnp.float32)
    attended = attended.reshape(length, width).astype(jnp.bfloat16)
    hidden = inputs + matmul(attended, output_weight)
    normed_second = rms_scale(hidden, gain_second).astype(jnp.bfloat16)
    logits = matmul(normed_second, router_weight)
    chances = jax.nn.softmax(logits, axis=-1)
    picks = (routes == lax.broadcasted_iota(jnp.int32, (1, experts), 1)).astype(jnp.float32)
    gate = jnp.sum(chances * picks, axis=1, keepdims=True)
    lower = (
        lax.broadcasted_iota(jnp.int32, (length, length), 0)
        > lax.broadcasted_iota(jnp.int32, (length, length), 1)
    ).astype(jnp.bfloat16)
    earlier = matmul(lower, picks.astype(jnp.bfloat16))
    slots = jnp.sum(earlier * picks, axis=1).astype(jnp.int32)
    place = routes[:, 0] * capacity + slots
    dispatch = (
        place[:, None] == lax.broadcasted_iota(jnp.int32, (1, experts * capacity), 1)
    ).astype(jnp.bfloat16)
    outgoing = transposed_times(dispatch, normed_second).astype(jnp.bfloat16)
    arrived = lax.all_to_all(outgoing, "expert", split_axis=0, concat_axis=0, tiled=True)
    upstream = cotangent.astype(jnp.float32)
    returned_grad = (gate * upstream).astype(jnp.bfloat16)
    outgoing_grad = transposed_times(dispatch, returned_grad).astype(jnp.bfloat16)
    result_grad = lax.all_to_all(outgoing_grad, "expert", split_axis=0, concat_axis=0, tiled=True)
    paired_grad = lax.all_gather(result_grad, "wshard", axis=0, tiled=True)
    inner = w_in[0]
    outer = w_out[0]
    paired = lax.all_gather(arrived, "wshard", axis=0, tiled=True)
    before = matmul(paired, inner)
    active = smooth(before).astype(jnp.bfloat16)
    result = lax.psum_scatter(matmul(active, outer), "wshard", scatter_dimension=0, tiled=True)
    returned = lax.all_to_all(
        result.astype(jnp.bfloat16), "expert", split_axis=0, concat_axis=0, tiled=True
    )
    expert_out = matmul(dispatch, returned)
    output = hidden + gate * expert_out
    gate_grad = jnp.sum(upstream * expert_out, axis=1, keepdims=True)
    active_grad = times_transposed(paired_grad, outer)
    before_grad = jax.vjp(smooth, before)[1](active_grad)[0].astype(jnp.bfloat16)
    outer_grad = transposed_times(active, paired_grad)
    inner_grad = transposed_times(paired, before_grad)
    arrived_grad = lax.psum_scatter(
        times_transposed(before_grad, inner), "wshard", scatter_dimension=0, tiled=True
    )
    grad_inner = inner_grad[None]
    grad_outer = outer_grad[None]
    sent_grad = lax.all_to_all(
        arrived_grad.astype(jnp.bfloat16), "expert", split_axis=0, concat_axis=0, tiled=True
    )
    normed_second_grad = matmul(dispatch, sent_grad)
    logit_grad = (chances * (picks - gate) * gate_grad).astype(jnp.bfloat16)
    router_grad = transposed_times(normed_second, logit_grad)
    normed_second_grad = normed_second_grad + times_transposed(logit_grad, router_weight)
    hidden_part, gain_second_grad = jax.vjp(rms_scale, hidden, gain_second)[1](normed_second_grad)
    hidden_grad = upstream + hidden_part
    hidden_low = hidden_grad.astype(jnp.bfloat16)
    output_grad = transposed_times(attended, hidden_low)
    attended_grad = (
        times_transposed(hidden_low, output_weight)
        .astype(jnp.bfloat16)
        .reshape(length, heads, head_size)
    )
    scores = score_of()
    probs = jnp.exp(scores - log_total)
    probs_low = probs.astype(jnp.bfloat16)
    value_grad = jnp.einsum(
        "hij,ihd->jhd", probs_low, attended_grad, preferred_element_type=jnp.float32
    )
    value_grad = value_grad.astype(jnp.bfloat16).reshape(length, width)
    probs_grad = jnp.einsum(
        "ihd,jhd->hij", attended_grad, value_low, preferred_element_type=jnp.float32
    )
    score_grad = (
        probs * (probs_grad - jnp.sum(probs_grad * probs, axis=-1, keepdims=True))
    ).astype(jnp.bfloat16)
    table_grad = jnp.einsum(
        "bij,hij->bh", bucket_hits, score_grad, preferred_element_type=jnp.float32
    )
    query_grad = (
        jnp.einsum("hij,jhd->ihd", score_grad, key_low, preferred_element_type=jnp.float32) * factor
    )
    query_grad = query_grad.astype(jnp.bfloat16).reshape(length, width)
    key_grad = (
        jnp.einsum("hij,ihd->jhd", score_grad, query_low, preferred_element_type=jnp.float32)
        * factor
    )
    key_grad = key_grad.astype(jnp.bfloat16).reshape(length, width)
    query_weight_grad = transposed_times(normed_first, query_grad)
    key_weight_grad = transposed_times(normed_first, key_grad)
    value_weight_grad = transposed_times(normed_first, value_grad)
    normed_first_grad = (
        times_transposed(query_grad, query_weight)
        + times_transposed(key_grad, key_weight)
        + times_transposed(value_grad, value_weight)
    )
    input_part, gain_first_grad = jax.vjp(rms_scale, inputs, gain_first)[1](normed_first_grad)
    input_grad = hidden_grad + input_part
    large = jnp.stack([query_weight_grad, key_weight_grad, value_weight_grad, output_grad])
    large = lax.psum_scatter(
        large.astype(jnp.bfloat16), "wshard", scatter_dimension=1, tiled=True
    )
    large = lax.psum(large, "expert").astype(jnp.float32)
    small = jnp.concatenate(
        [
            router_grad.reshape(-1),
            gain_first_grad,
            gain_second_grad,
            table_grad.reshape(-1),
        ]
    )
    small = lax.psum(small, ("expert", "wshard"))
    side = lax.axis_index("wshard")
    half = width // lax.axis_size("wshard")
    half_table = buckets // lax.axis_size("wshard")
    cuts = (width * experts, width * experts + width, width * experts + 2 * width)
    router_all, first_all, second_all, table_all = jnp.split(small, cuts)
    router_all = router_all.reshape(width, experts)
    table_all = table_all.reshape(buckets, heads)

    def own(array, size):
        return lax.dynamic_slice_in_dim(array, side * size, size, 0)

    totals = (
        own(first_all, half),
        large[0],
        large[1],
        large[2],
        large[3],
        own(table_all, half_table),
        own(second_all, half),
        own(router_all, half),
    )
    return (
        output.astype(jnp.bfloat16),
        input_grad,
        totals[0],
        totals[1],
        totals[2],
        totals[3],
        totals[4],
        totals[5],
        totals[6],
        totals[7],
        grad_inner,
        grad_outer,
    )


def solution(mesh):
    in_specs = (
        P(("expert", "wshard"), None),
        P("wshard"),
        P("wshard", None),
        P("wshard", None),
        P("wshard", None),
        P("wshard", None),
        P("wshard", None),
        P("wshard"),
        P("wshard", None),
        P("expert", None, "wshard"),
        P("expert", "wshard", None),
        P(("expert", "wshard"), None),
        P(("expert", "wshard"), None),
        P(("expert", "wshard"), None),
    )
    out_specs = (
        P(("expert", "wshard"), None),
        P(("expert", "wshard"), None),
        P("wshard"),
        P("wshard", None),
        P("wshard", None),
        P("wshard", None),
        P("wshard", None),
        P("wshard", None),
        P("wshard"),
        P("wshard", None),
        P("expert", None, "wshard"),
        P("expert", "wshard", None),
    )
    return jax.shard_map(
        per_device, mesh=mesh, in_specs=in_specs, out_specs=out_specs, check_vma=False
    )
```

```python
import functools

import jax
import jax.numpy as jnp
from jax import lax
from jax.experimental import pallas as pl
from jax.experimental.pallas import tpu as pltpu
from jax.sharding import PartitionSpec as P

bucket_edges = (12, 16, 23, 32, 46, 64, 91)
mask_fill = -1e30
norm_eps = 1e-06


def rms_scale(value, gain):
    return value * lax.rsqrt(jnp.mean(value * value, axis=-1, keepdims=True) + norm_eps) * gain


def smooth(value):
    return jax.nn.gelu(value, approximate=True)


def matmul(left, right):
    return jnp.dot(left, right, preferred_element_type=jnp.float32)


def times_transposed(left, right):
    return lax.dot_general(
        left, right, (((1,), (1,)), ((), ())), preferred_element_type=jnp.float32
    )


def transposed_times(left, right):
    return lax.dot_general(
        left, right, (((0,), (0,)), ((), ())), preferred_element_type=jnp.float32
    )


def bucket_grid(length):
    query_pos = lax.broadcasted_iota(jnp.int32, (length, length), 0)
    memory_pos = lax.broadcasted_iota(jnp.int32, (length, length), 1)
    offset = memory_pos - query_pos
    distance = jnp.abs(offset)
    beyond = 8 + sum(((distance >= edge).astype(jnp.int32) for edge in bucket_edges))
    upper = jnp.where(offset > 0, 16, 0).astype(jnp.int32)
    return upper + jnp.where(distance < 8, distance, beyond)


def segment_of(lengths, length):
    count = lengths.shape[0]
    upto = lax.broadcasted_iota(jnp.int32, (count, count), 0) <= lax.broadcasted_iota(
        jnp.int32, (count, count), 1
    )
    ends = jnp.sum(jnp.where(upto, lengths[:, None], 0), axis=0)
    places = lax.broadcasted_iota(jnp.int32, (length, 1), 0)
    return jnp.sum((places >= ends[None, :]).astype(jnp.int32), axis=1)


def sum_kernel(
    bits,
    query_ref,
    key_ref,
    value_ref,
    output_ref,
    small_ref,
    query_out,
    key_out,
    value_out,
    output_out,
    small_out,
    total,
    near,
    send,
    recv,
    done,
    small_mine,
    small_theirs,
    near_sems,
    down_sems,
    up_sems,
    small_sems,
):
    expert = lax.axis_index("expert")
    side = lax.axis_index("wshard")
    parts, rows, columns = total.shape
    half = query_out.shape[0]
    orders = [[(p + i) % 3 for i in range(3)] + list(range(3, bits)) for p in range(parts)]

    def across(bit):
        place = lax.rem(expert // (1 << bit), 2)
        return (expert + (1 - 2 * place) * (1 << bit), side), place

    other = (expert, 1 - side)
    barrier = pltpu.get_barrier_semaphore()
    for peer in [other] + [across(bit)[0] for bit in range(bits)]:
        pl.semaphore_signal(
            barrier, inc=1, device_id=peer, device_id_type=pl.DeviceIdType.MESH
        )
    pl.semaphore_wait(barrier, bits + 1)

    def remote(source, target, sems, peer):
        return pltpu.make_async_remote_copy(
            src_ref=source,
            dst_ref=target,
            send_sem=sems.at[0],
            recv_sem=sems.at[1],
            device_id=peer,
            device_id_type=pl.DeviceIdType.MESH,
        )

    given = (query_ref, key_ref, value_ref, output_ref)
    waiting = []
    theirs = pl.ds(pl.multiple_of((1 - side) * half, 16), half)
    mine = pl.ds(pl.multiple_of(side * half, 16), half)
    first = []
    for m, ref in enumerate(given):
        copy = remote(ref.at[theirs, :], near.at[m], near_sems.at[m], other)
        copy.start()
        first.append(copy)
    small_mine[0] = small_ref[...]
    small_copy = remote(small_mine.at[0], small_theirs.at[0], small_sems.at[0], other)
    small_copy.start()

    span = [0]

    def fill(upto):
        while span[0] < upto:
            t = span[0]
            m, c = t // 2, t % 2
            if c == 0:
                first[m].wait()
            cut = slice(c * columns, (c + 1) * columns)
            piece = given[m][mine, cut].astype(jnp.float32) + near[m, :, cut].astype(jnp.float32)
            low, high = t * half, (t + 1) * half
            at = low
            while at < high:
                p = at // rows
                stop = min(high, (p + 1) * rows)
                total[p, at - p * rows : stop - p * rows, :] = piece[at - low : stop - low]
                at = stop
            span[0] = t + 1

    offsets = [0] * parts
    flying = [None] * parts
    keeps = [None] * parts
    length = rows
    lead = 0
    pieces = parts * rows // half
    for level in range(bits + 1):
        for p in range(parts):
            if level == 0:
                fill(min(pieces, -(-(p + 1) * rows // half)))
            else:
                flying[p].wait()
                keep = keeps[p]
                total[p, keep, :] = total[p, keep, :] + recv[
                    p, lead - length : lead, :
                ].astype(jnp.float32)
            if level < bits:
                peer, place = across(orders[p][level])
                step = length // 2
                away = pl.ds(pl.multiple_of(offsets[p] + (1 - place) * step, 16), step)
                offsets[p] = offsets[p] + place * step
                keeps[p] = pl.ds(pl.multiple_of(offsets[p], 16), step)
                send[p, lead : lead + step, :] = total[p, away, :].astype(jnp.bfloat16)
                flying[p] = remote(
                    send.at[p, lead : lead + step, :],
                    recv.at[p, lead : lead + step, :],
                    down_sems.at[p, level],
                    peer,
                )
                flying[p].start()
            else:
                done[p, keeps[p], :] = total[p, keeps[p], :].astype(jnp.bfloat16)
                peer, place = across(orders[p][bits - 1])
                flying[p] = remote(
                    done.at[p, keeps[p], :],
                    done.at[p, keeps[p], :],
                    up_sems.at[p, bits - 1],
                    peer,
                )
                flying[p].start()
        small_copy.wait()
        small_mine[level + 1] = small_mine[level] + small_theirs[level]
        if level < bits:
            small_copy = remote(
                small_mine.at[level + 1],
                small_theirs.at[level + 1],
                small_sems.at[level + 1],
                across(level)[0],
            )
            small_copy.start()
            length = length // 2
            lead = lead + length
    small_out[...] = small_mine[bits + 1]
    for level in range(bits - 1, -1, -1):
        for p in range(parts):
            flying[p].wait()
            peer, place = across(orders[p][level])
            offsets[p] = offsets[p] - place * length
            if level > 0:
                peer, place = across(orders[p][level - 1])
                held = pl.ds(pl.multiple_of(offsets[p], 16), 2 * length)
                flying[p] = remote(
                    done.at[p, held, :], done.at[p, held, :], up_sems.at[p, level - 1], peer
                )
                flying[p].start()
        length = 2 * length
    for t in range(pieces):
        m, c = t // 2, t % 2
        out = (query_out, key_out, value_out, output_out)[m]
        low, high = t * half, (t + 1) * half
        at = low
        while at < high:
            p = at // rows
            stop = min(high, (p + 1) * rows)
            out[at - low : stop - low, c * columns : (c + 1) * columns] = done[
                p, at - p * rows : stop - p * rows, :
            ].astype(jnp.float32)
            at = stop


def sum_over_devices(query, key, value, output, small):
    bits = (lax.axis_size("expert") - 1).bit_length()
    width = query.shape[0]
    half = width // lax.axis_size("wshard")
    parts, columns = 3, width // 2
    rows = 4 * half * width // (parts * columns)
    vmem = pl.BlockSpec(memory_space=pltpu.VMEM)
    return pl.pallas_call(
        functools.partial(sum_kernel, bits),
        out_shape=[jax.ShapeDtypeStruct((half, width), jnp.float32)] * 4
        + [jax.ShapeDtypeStruct(small.shape, jnp.float32)],
        in_specs=[vmem] * 5,
        out_specs=[vmem] * 5,
        scratch_shapes=[
            pltpu.VMEM((parts, rows, columns), jnp.float32),
            pltpu.VMEM((4, half, width), jnp.bfloat16),
            pltpu.VMEM((parts, rows, columns), jnp.bfloat16),
            pltpu.VMEM((parts, rows, columns), jnp.bfloat16),
            pltpu.VMEM((parts, rows, columns), jnp.bfloat16),
            pltpu.VMEM((bits + 2,) + small.shape, jnp.float32),
            pltpu.VMEM((bits + 1,) + small.shape, jnp.float32),
            pltpu.SemaphoreType.DMA((4, 2)),
            pltpu.SemaphoreType.DMA((parts, bits, 2)),
            pltpu.SemaphoreType.DMA((parts, bits, 2)),
            pltpu.SemaphoreType.DMA((bits + 1, 2)),
        ],
        compiler_params=pltpu.CompilerParams(
            collective_id=0, has_side_effects=True, vmem_limit_bytes=48 * 1024 * 1024
        ),
    )(query, key, value, output, small)


def per_device(
    tokens,
    norm1_gain,
    w_query,
    w_key,
    w_value,
    w_output,
    rel_bias,
    norm2_gain,
    w_router,
    w_in,
    w_out,
    seq_lens,
    routes,
    cotangent,
):
    gathered = (
        lax.all_gather(norm1_gain, "wshard", axis=0, tiled=True),
        lax.all_gather(w_query, "wshard", axis=0, tiled=True),
        lax.all_gather(w_key, "wshard", axis=0, tiled=True),
        lax.all_gather(w_value, "wshard", axis=0, tiled=True),
        lax.all_gather(w_output, "wshard", axis=0, tiled=True),
        lax.all_gather(rel_bias, "wshard", axis=0, tiled=True),
        lax.all_gather(norm2_gain, "wshard", axis=0, tiled=True),
        lax.all_gather(w_router, "wshard", axis=0, tiled=True),
    )
    (
        gain_first,
        query_weight,
        key_weight,
        value_weight,
        output_weight,
        bias_table,
        gain_second,
        router_weight,
    ) = gathered
    gain_first = gain_first.astype(jnp.float32)
    gain_second = gain_second.astype(jnp.float32)
    length, width = tokens.shape
    buckets, heads = bias_table.shape
    head_size = width // heads
    factor = head_size ** (-0.5)
    experts = router_weight.shape[1]
    capacity = max(2, 3 * length // (2 * experts))
    inputs = tokens.astype(jnp.float32)
    grid = bucket_grid(length)
    bucket_hits = (grid[None] == lax.broadcasted_iota(jnp.int32, (buckets, 1, 1), 0)).astype(
        jnp.bfloat16
    )
    segment = segment_of(seq_lens[0], length)
    same = (segment[:, None] == segment[None, :])[None]
    position_bias = jnp.einsum(
        "bij,bh->hij", bucket_hits, bias_table, preferred_element_type=jnp.float32
    )
    normed_first = rms_scale(inputs, gain_first).astype(jnp.bfloat16)
    query_low = (
        matmul(normed_first, query_weight).astype(jnp.bfloat16).reshape(length, heads, head_size)
    )
    key_low = (
        matmul(normed_first, key_weight).astype(jnp.bfloat16).reshape(length, heads, head_size)
    )
    value_low = (
        matmul(normed_first, value_weight).astype(jnp.bfloat16).reshape(length, heads, head_size)
    )

    def score_of():
        raw = (
            jnp.einsum("ihd,jhd->hij", query_low, key_low, preferred_element_type=jnp.float32)
            * factor
            + position_bias
        )
        return jnp.where(same, raw, mask_fill)

    scores = score_of()
    peak = jnp.max(scores, axis=-1, keepdims=True)
    lifted = jnp.exp(scores - peak)
    totals_row = jnp.sum(lifted, axis=-1, keepdims=True)
    probs = lifted / totals_row
    log_total = peak + jnp.log(totals_row)
    probs_low = probs.astype(jnp.bfloat16)
    attended = jnp.einsum("hij,jhd->ihd", probs_low, value_low, preferred_element_type=jnp.float32)
    attended = attended.reshape(length, width).astype(jnp.bfloat16)
    hidden = inputs + matmul(attended, output_weight)
    normed_second = rms_scale(hidden, gain_second).astype(jnp.bfloat16)
    logits = matmul(normed_second, router_weight)
    chances = jax.nn.softmax(logits, axis=-1)
    picks = (routes == lax.broadcasted_iota(jnp.int32, (1, experts), 1)).astype(jnp.float32)
    gate = jnp.sum(chances * picks, axis=1, keepdims=True)
    lower = (
        lax.broadcasted_iota(jnp.int32, (length, length), 0)
        > lax.broadcasted_iota(jnp.int32, (length, length), 1)
    ).astype(jnp.bfloat16)
    earlier = matmul(lower, picks.astype(jnp.bfloat16))
    slots = jnp.sum(earlier * picks, axis=1).astype(jnp.int32)
    place = routes[:, 0] * capacity + slots
    dispatch = (
        place[:, None] == lax.broadcasted_iota(jnp.int32, (1, experts * capacity), 1)
    ).astype(jnp.bfloat16)
    outgoing = transposed_times(dispatch, normed_second).astype(jnp.bfloat16)
    arrived = lax.all_to_all(outgoing, "expert", split_axis=0, concat_axis=0, tiled=True)
    upstream = cotangent.astype(jnp.float32)
    returned_grad = (gate * upstream).astype(jnp.bfloat16)
    outgoing_grad = transposed_times(dispatch, returned_grad).astype(jnp.bfloat16)
    result_grad = lax.all_to_all(outgoing_grad, "expert", split_axis=0, concat_axis=0, tiled=True)
    paired_grad = lax.all_gather(result_grad, "wshard", axis=0, tiled=True)
    inner = w_in[0]
    outer = w_out[0]
    paired = lax.all_gather(arrived, "wshard", axis=0, tiled=True)
    before = matmul(paired, inner)
    active = smooth(before).astype(jnp.bfloat16)
    result = lax.psum_scatter(matmul(active, outer), "wshard", scatter_dimension=0, tiled=True)
    returned = lax.all_to_all(
        result.astype(jnp.bfloat16), "expert", split_axis=0, concat_axis=0, tiled=True
    )
    expert_out = matmul(dispatch, returned)
    output = hidden + gate * expert_out
    gate_grad = jnp.sum(upstream * expert_out, axis=1, keepdims=True)
    active_grad = times_transposed(paired_grad, outer)
    before_grad = jax.vjp(smooth, before)[1](active_grad)[0].astype(jnp.bfloat16)
    outer_grad = transposed_times(active, paired_grad)
    inner_grad = transposed_times(paired, before_grad)
    arrived_grad = lax.psum_scatter(
        times_transposed(before_grad, inner), "wshard", scatter_dimension=0, tiled=True
    )
    grad_inner = inner_grad[None]
    grad_outer = outer_grad[None]
    sent_grad = lax.all_to_all(
        arrived_grad.astype(jnp.bfloat16), "expert", split_axis=0, concat_axis=0, tiled=True
    )
    normed_second_grad = matmul(dispatch, sent_grad)
    logit_grad = (chances * (picks - gate) * gate_grad).astype(jnp.bfloat16)
    router_grad = transposed_times(logit_grad, normed_second)
    normed_second_grad = normed_second_grad + times_transposed(logit_grad, router_weight)
    hidden_part, gain_second_grad = jax.vjp(rms_scale, hidden, gain_second)[1](normed_second_grad)
    hidden_grad = upstream + hidden_part
    hidden_low = hidden_grad.astype(jnp.bfloat16)
    output_grad = transposed_times(attended, hidden_low)
    attended_grad = (
        times_transposed(hidden_low, output_weight)
        .astype(jnp.bfloat16)
        .reshape(length, heads, head_size)
    )
    scores = score_of()
    probs = jnp.exp(scores - log_total)
    probs_low = probs.astype(jnp.bfloat16)
    value_grad = jnp.einsum(
        "hij,ihd->jhd", probs_low, attended_grad, preferred_element_type=jnp.float32
    )
    value_grad = value_grad.astype(jnp.bfloat16).reshape(length, width)
    probs_grad = jnp.einsum(
        "ihd,jhd->hij", attended_grad, value_low, preferred_element_type=jnp.float32
    )
    score_grad = (
        probs * (probs_grad - jnp.sum(probs_grad * probs, axis=-1, keepdims=True))
    ).astype(jnp.bfloat16)
    table_grad = jnp.einsum(
        "bij,hij->bh", bucket_hits, score_grad, preferred_element_type=jnp.float32
    )
    query_grad = (
        jnp.einsum("hij,jhd->ihd", score_grad, key_low, preferred_element_type=jnp.float32) * factor
    )
    query_grad = query_grad.astype(jnp.bfloat16).reshape(length, width)
    key_grad = (
        jnp.einsum("hij,ihd->jhd", score_grad, query_low, preferred_element_type=jnp.float32)
        * factor
    )
    key_grad = key_grad.astype(jnp.bfloat16).reshape(length, width)
    query_weight_grad = transposed_times(normed_first, query_grad)
    key_weight_grad = transposed_times(normed_first, key_grad)
    value_weight_grad = transposed_times(normed_first, value_grad)
    normed_first_grad = (
        times_transposed(query_grad, query_weight)
        + times_transposed(key_grad, key_weight)
        + times_transposed(value_grad, value_weight)
    )
    input_part, gain_first_grad = jax.vjp(rms_scale, inputs, gain_first)[1](normed_first_grad)
    input_grad = hidden_grad + input_part
    bias_rows = -(-buckets * heads // width)
    used = experts + 2 + bias_rows
    bias_flat = jnp.pad(table_grad.reshape(-1), (0, bias_rows * width - buckets * heads))
    small = jnp.concatenate(
        [
            router_grad,
            gain_first_grad[None],
            gain_second_grad[None],
            bias_flat.reshape(bias_rows, width),
            jnp.zeros((-used % 8, width), jnp.float32),
        ]
    )
    large = sum_over_devices(
        query_weight_grad.astype(jnp.bfloat16),
        key_weight_grad.astype(jnp.bfloat16),
        value_weight_grad.astype(jnp.bfloat16),
        output_grad.astype(jnp.bfloat16),
        small,
    )
    side = lax.axis_index("wshard")
    half = width // lax.axis_size("wshard")
    half_table = buckets // lax.axis_size("wshard")
    small = large[4]
    router_all = small[:experts]
    first_all = small[experts]
    second_all = small[experts + 1]
    table_all = small[experts + 2 : used].reshape(-1)[: buckets * heads].reshape(buckets, heads)

    def own(array, size, axis=0):
        return lax.dynamic_slice_in_dim(array, side * size, size, axis)

    totals = (
        own(first_all, half),
        large[0],
        large[1],
        large[2],
        large[3],
        own(table_all, half_table),
        own(second_all, half),
        own(router_all, half, 1).T,
    )
    return (
        output.astype(jnp.bfloat16),
        input_grad,
        totals[0],
        totals[1],
        totals[2],
        totals[3],
        totals[4],
        totals[5],
        totals[6],
        totals[7],
        grad_inner,
        grad_outer,
    )


def solution(mesh):
    in_specs = (
        P(("expert", "wshard"), None),
        P("wshard"),
        P("wshard", None),
        P("wshard", None),
        P("wshard", None),
        P("wshard", None),
        P("wshard", None),
        P("wshard"),
        P("wshard", None),
        P("expert", None, "wshard"),
        P("expert", "wshard", None),
        P(("expert", "wshard"), None),
        P(("expert", "wshard"), None),
        P(("expert", "wshard"), None),
    )
    out_specs = (
        P(("expert", "wshard"), None),
        P(("expert", "wshard"), None),
        P("wshard"),
        P("wshard", None),
        P("wshard", None),
        P("wshard", None),
        P("wshard", None),
        P("wshard", None),
        P("wshard"),
        P("wshard", None),
        P("expert", None, "wshard"),
        P("expert", "wshard", None),
    )
    return jax.shard_map(
        per_device, mesh=mesh, in_specs=in_specs, out_specs=out_specs, check_vma=False
    )
```
